512 devices in a mesh: seq: 64 (over z_lo, x, y), tp: 8 (over z_hi, core).
Axes of the slice: x: 4, y: 8, z: 8 (z_hi: 4, z_lo: 2; z = z_hi * 2 + z_lo), core: 2. Of those that a mesh axis runs over, the one named last changes fastest.
Arguments:
- hidden: bfloat16 [65536, 8192], P('seq', 'tp'), may hold values from -6 to 6
- keep_first: int32 [64, 512], P('seq'), may hold values from 0 to 1023, as said below
- keep_second: int32 [16384], P('seq'), may hold values from 0 to 1023, as said below
- norm_gain: float32 [8192], replicated, may hold values from 0.1 to 1.9
- w_query: bfloat16 [8192, 4096], P('seq', 'tp'), may hold values from -1.3479223 to 1.3479223
- w_keyval: bfloat16 [8192, 2, 1024], P('seq', None, 'tp'), may hold values from -0.0508233 to 0.0508233
Outputs:
- attended: bfloat16 [16384, 4096], P('seq', 'tp')
The draws below stay inside these ranges and needn't reach their ends.
Inputs may be any that keep to these rules, and one draw needn't show every extreme that they name: `keep_first`: each row lists 512 distinct positions in increasing order, the last being 1023. `keep_second`: each aligned run of 512 entries lists distinct positions of one merged pair in increasing order, the last being 1023.
All inputs are finite; a program needn't handle non-finite values.
Results may differ from the reference program's by a relative error of at most 0.0081.
Values may be sent and summed in bfloat16 or wider, within the bound.
A program may use at most 64 MiB of HBM per device.

```python
import math
import jax
import jax.numpy as jnp
from jax import lax

D = 8192
HD = 128
QH = 32
KVH = 8
SPAN = 1024
SPANS = 64
TOKENS = 65536
KEEP1 = 512
MROWS = 16384


def clipped_normal(key, shape):
    return jnp.clip(jax.random.normal(key, shape, jnp.float32), -4.5, 4.5) * D ** (-0.5)


def key_weights(key):
    return clipped_normal(key, (D, KVH * HD))


def pick_sorted(row_key, count, length):
    chosen = jax.random.permutation(row_key, length - 1)[:count - 1].astype(jnp.int32)
    return jnp.sort(jnp.concatenate([chosen, jnp.full((1,), length - 1, jnp.int32)]))


def pick_kept(row_key):
    return pick_sorted(row_key, KEEP1, SPAN)


def draw_keep_first(key, part):
    key = jax.random.fold_in(key, 3)
    row_keys = jax.random.split(key, SPANS)
    return jax.vmap(pick_kept)(row_keys)


def draw_keep_second(key, part):
    key = jax.random.fold_in(key, 4)
    row_keys = jax.random.split(key, SPANS // 2)
    return jax.vmap(pick_kept)(row_keys).reshape(MROWS)


def draw_w_keyval(key, part):
    base_keys = key_weights(key)
    key = jax.random.fold_in(key, 5)
    values = clipped_normal(key, (D, KVH * HD))
    return jnp.stack([base_keys, values], axis=1).astype(jnp.bfloat16)


def draw_w_query(key, part):
    key = jax.random.fold_in(key, 6)
    result = clipped_normal(key, (D, QH * HD))
    return result.astype(jnp.bfloat16)


def block_scale(own_key, dims, pieces, least, top_value):
    loudness, own = 1.0, jax.random.fold_in(own_key, 6)
    for axis_at, shards_of in pieces:
        heights = jnp.exp(jax.random.uniform(jax.random.fold_in(own, axis_at), (shards_of,), jnp.float32, least / len(pieces), top_value / len(pieces)))
        loudness = loudness * jnp.repeat(heights, dims[axis_at] // shards_of).reshape([-1 if axis == axis_at else 1 for axis in range(len(dims))])
    return loudness


def bell_draw(own_key, extent, scale, bound, pieces=(), kind=jnp.bfloat16):
    gain = block_scale(own_key, extent, pieces, -0.22, 0.18) if pieces else 1.0
    array = jax.random.normal(own_key, extent, jnp.float32) * scale * gain
    return jnp.minimum(jnp.maximum(array, -bound), bound).astype(kind)


def setup_inputs(seed: int = 0) -> dict:
    keys = jax.random.split(jax.random.key(seed), 7)
    hidden = bell_draw(keys[0], (TOKENS, D), 1.0, 6.0, ((0, 64), (1, 8)))
    keep_first = draw_keep_first(jax.random.fold_in(keys[6], 71), 0)
    keep_second = draw_keep_second(jax.random.fold_in(keys[6], 71), 0)
    norm_gain = jnp.clip(1.0 + 0.18 * jax.random.normal(keys[3], (D,), jnp.float32), 0.1, 1.9)
    w_query = draw_w_query(jax.random.fold_in(keys[6], 71), 0)
    w_keyval = draw_w_keyval(jax.random.fold_in(keys[6], 71), 0)
    return dict(hidden=hidden, keep_first=keep_first, keep_second=keep_second, norm_gain=norm_gain, w_query=w_query, w_keyval=w_keyval)


eps = 1e-05

def rotate(values, positions):
    half_dim = values.shape[-1] // 2
    frequency = jnp.exp(jnp.arange(half_dim, dtype=jnp.float32) * (-2.0 * math.log(10000.0) / values.shape[-1]))
    angles = positions.astype(jnp.float32)[:, None] * frequency[None, :]
    cosine = jnp.cos(angles)[:, None, :]
    sine_part = jnp.sin(angles)[:, None, :]
    first_half = values[..., :half_dim]
    second_half = values[..., half_dim:]
    return jnp.concatenate([first_half * cosine - second_half * sine_part, second_half * cosine + first_half * sine_part], axis=-1)

def attend(blocks_in):
    quad_query, quad_keys, quad_values = blocks_in
    grouped = quad_query.astype(jnp.float32).reshape(SPAN, KVH, QH // KVH, HD)
    scores = jnp.einsum('qkgd,ckd->kgqc', grouped, quad_keys.astype(jnp.float32)) / math.sqrt(HD)
    causal = jnp.arange(SPAN)[:, None] >= jnp.arange(SPAN)[None, :]
    scores = jnp.where(causal, scores, -jnp.inf)
    row_max = lax.optimization_barrier(jnp.max(scores, axis=-1, keepdims=True))
    weights = jnp.exp(scores - row_max)
    weights = (weights / lax.optimization_barrier(jnp.sum(weights, axis=-1, keepdims=True))).astype(jnp.bfloat16)
    result = jnp.einsum('kgqc,ckd->qkgd', weights.astype(jnp.float32), quad_values.astype(jnp.float32))
    return result.reshape(SPAN, QH * HD).astype(jnp.bfloat16)

def reference(hidden, keep_first, keep_second, norm_gain, w_query, w_keyval):
    spans = hidden.reshape(SPANS, SPAN, D)
    kept_rows = jnp.take_along_axis(spans, keep_first.astype(jnp.int32)[:, :, None], axis=1)
    paired = kept_rows.reshape(SPANS // 2, SPAN, D)
    second_picks = keep_second.astype(jnp.int32).reshape(SPANS // 2, KEEP1)
    merged = jnp.take_along_axis(paired, second_picks[:, :, None], axis=1).reshape(MROWS, D)
    widened = merged.astype(jnp.float32)
    inv_rms = lax.rsqrt(lax.optimization_barrier(jnp.mean(widened * widened, axis=1, keepdims=True)) + eps)
    normed = (widened * inv_rms * norm_gain[None, :]).astype(jnp.bfloat16)
    query = jnp.dot(normed, w_query, preferred_element_type=jnp.float32)
    keyval = jnp.dot(normed, w_keyval.reshape(D, 2 * KVH * HD), preferred_element_type=jnp.float32)
    positions = (jnp.arange(MROWS) % SPAN).astype(jnp.int32)
    rot_query = rotate(query.reshape(MROWS, QH, HD), positions).astype(jnp.bfloat16)
    keyval = keyval.reshape(MROWS, 2, KVH, HD)
    rot_keys = rotate(keyval[:, 0], positions).astype(jnp.bfloat16)
    values = keyval[:, 1].astype(jnp.bfloat16)
    quad_count = MROWS // SPAN
    attended = lax.map(attend, (rot_query.reshape(quad_count, SPAN, QH, HD), rot_keys.reshape(quad_count, SPAN, KVH, HD), values.reshape(quad_count, SPAN, KVH, HD)))
    return attended.reshape(MROWS, QH * HD)
```

```python
import math

import jax
import jax.numpy as jnp
from jax import lax
from jax.experimental import pallas as pl
from jax.experimental.pallas import tpu as pltpu
from jax.sharding import PartitionSpec as P

HD = 128
NX, NY = 4, 8
MESH = pl.DeviceIdType.MESH
X_RIGHT, X_LEFT, Y_RIGHT, Y_LEFT, Z_OTHER = (1, 0, 0), (-1, 0, 0), (0, 1, 0), (0, -1, 0), (0, 0, 1)

eps = 1e-05


def from_partner(block, axis, stride):
    count = lax.axis_size(axis)
    route = []
    for low in range(count):
        high = low | 1 << stride
        if high != low and high < count:
            route += [(low, high), (high, low)]
    return lax.ppermute(block, axis, route)


def gather_weights(wq_ref, wkv_ref, q_all, kv_all, send_sems, recv_sems, local_sems):
    me = lax.axis_index("seq")
    tp = lax.axis_index("tp")
    zl, x, y = me // (NX * NY), me // NY % NX, me % NY

    def device(way):
        dx, dy, dz = way
        nx, ny, nz = lax.rem(x + dx + NX, NX), lax.rem(y + dy + NY, NY), lax.rem(zl + dz, 2)
        return (nz * (NX * NY) + nx * NY + ny, tp)

    def at(ref, other, xo, yo):
        plane = lax.rem(zl + other, 2)
        row = lax.rem(y + yo + 2 * NY, NY)
        if xo is None:
            return ref.at[plane, :, row]
        return ref.at[plane, lax.rem(x + xo + 2 * NX, NX), row]

    barrier = pltpu.get_barrier_semaphore()
    for way in (X_RIGHT, X_LEFT, Y_RIGHT, Y_LEFT, Z_OTHER):
        pl.semaphore_signal(barrier, inc=1, device_id=device(way), device_id_type=MESH)
    pl.semaphore_wait(barrier, 5)

    mine_q = pltpu.make_async_copy(wq_ref, at(q_all, 0, 0, 0), local_sems.at[0])
    mine_kv = pltpu.make_async_copy(wkv_ref, at(kv_all, 0, 0, 0), local_sems.at[1])
    mine_q.start()
    mine_kv.start()

    copies = []
    table = {}

    def send(ref, way, other, xo, yo, src=None):
        number = len(copies)
        dst = at(ref, other, xo, yo)
        copy = pltpu.make_async_remote_copy(
            src_ref=dst if src is None else src,
            dst_ref=dst,
            send_sem=send_sems.at[number],
            recv_sem=recv_sems.at[number],
            device_id=device(way),
            device_id_type=MESH,
        )
        copy.start()
        copies.append(copy)
        dx, dy, dz = way
        there = (other + dz) % 2, None if xo is None else xo - dx, yo - dy
        landing = at(ref, *there)
        table[(id(ref), way) + there] = pltpu.make_async_remote_copy(
            src_ref=landing,
            dst_ref=landing,
            send_sem=send_sems.at[number],
            recv_sem=recv_sems.at[number],
            device_id=device(way),
            device_id_type=MESH,
        )

    def arrived(ref, way, other, xo, yo):
        table.pop((id(ref), way, other, xo, yo)).wait_recv()

    send(kv_all, Z_OTHER, 0, 0, 0, wkv_ref)
    send(q_all, Z_OTHER, 0, 0, 0, wq_ref)
    for way in (X_RIGHT, X_LEFT):
        send(kv_all, way, 0, 0, 0, wkv_ref)
    for way in (Y_RIGHT, Y_LEFT):
        send(q_all, way, 0, 0, 0, wq_ref)
    for way in (X_RIGHT, X_LEFT):
        send(q_all, way, 0, 0, 0, wq_ref)
    arrived(kv_all, Z_OTHER, 1, 0, 0)
    for way in (X_RIGHT, X_LEFT):
        send(kv_all, way, 1, 0, 0)
    arrived(q_all, Z_OTHER, 1, 0, 0)
    for way in (Y_RIGHT, Y_LEFT):
        send(q_all, way, 1, 0, 0)
    for way in (X_RIGHT, X_LEFT):
        send(q_all, way, 1, 0, 0)
    arrived(kv_all, X_RIGHT, 0, -1, 0)
    send(kv_all, X_RIGHT, 0, -1, 0)
    arrived(kv_all, X_LEFT, 1, 1, 0)
    send(kv_all, X_LEFT, 1, 1, 0)
    arrived(kv_all, X_LEFT, 0, 1, 0)
    arrived(kv_all, X_RIGHT, 1, -1, 0)
    mine_kv.wait()

    pending = [0]

    def second_hop(yo):
        arrived(q_all, X_RIGHT, 0, -1, yo)
        send(q_all, X_RIGHT, 0, -1, yo)
        arrived(q_all, X_LEFT, 1, 1, yo)
        send(q_all, X_LEFT, 1, 1, yo)

    def kv_hop(step):
        if step == 0:
            arrived(kv_all, X_RIGHT, 0, -2, 0)
            arrived(kv_all, X_LEFT, 1, 2, 0)
            for way in (Y_RIGHT, Y_LEFT):
                for other in (0, 1):
                    send(kv_all, way, other, None, 0)
            return
        for other in (0, 1):
            for way, sign, far in ((Y_RIGHT, -1, 4 - other), (Y_LEFT, 1, 3 + other)):
                if step <= far:
                    arrived(kv_all, way, other, None, sign * step)
                    if step < far:
                        send(kv_all, way, other, None, sign * step)

    def q_hop(step):
        for other in (0, 1):
            for way, sign, far in ((Y_RIGHT, -1, 4 - other), (Y_LEFT, 1, 3 + other)):
                if step <= far:
                    arrived(q_all, way, other, 0, sign * step)
                    if step < far:
                        send(q_all, way, other, 0, sign * step)
                    for side in (X_RIGHT, X_LEFT):
                        send(q_all, side, other, 0, sign * step)

    q_hop(1)
    kv_hop(0)
    second_hop(0)
    q_hop(2)
    second_hop(-1)
    second_hop(1)
    kv_hop(1)
    q_hop(3)
    second_hop(-2)
    kv_hop(2)
    second_hop(2)
    for other, way, sign in ((0, Y_RIGHT, -1), (1, Y_LEFT, 1)):
        arrived(q_all, way, other, 0, sign * 4)
        for side in (X_RIGHT, X_LEFT):
            send(q_all, side, other, 0, sign * 4)
    second_hop(-3)
    kv_hop(3)
    second_hop(3)
    arrived(q_all, X_RIGHT, 0, -1, -4)
    send(q_all, X_RIGHT, 0, -1, -4)
    arrived(q_all, X_LEFT, 1, 1, 4)
    send(q_all, X_LEFT, 1, 1, 4)
    kv_hop(4)
    for rest in list(table.values()):
        rest.wait_recv()
    mine_q.wait()
    for copy in copies:
        copy.wait_send()


COPIES = 84


def all_weights(w_query, w_keyval):
    rows, qc = w_query.shape
    kc = w_keyval.shape[1]
    return pl.pallas_call(
        gather_weights,
        out_shape=(
            jax.ShapeDtypeStruct((2, NX, NY, rows, qc), jnp.bfloat16),
            jax.ShapeDtypeStruct((2, NX, NY, rows, kc), jnp.bfloat16),
        ),
        in_specs=[pl.BlockSpec(memory_space=pl.ANY)] * 2,
        out_specs=(pl.BlockSpec(memory_space=pl.ANY),) * 2,
        scratch_shapes=[
            pltpu.SemaphoreType.DMA((COPIES,)),
            pltpu.SemaphoreType.DMA((COPIES,)),
            pltpu.SemaphoreType.DMA((2,)),
        ],
        compiler_params=pltpu.CompilerParams(collective_id=0, has_side_effects=True),
        cost_estimate=pl.CostEstimate(flops=0, bytes_accessed=200_000_000, transcendentals=0),
    )(w_query, w_keyval)


def rotate(values, positions):
    half_dim = values.shape[-1] // 2
    frequency = jnp.exp(
        jnp.arange(half_dim, dtype=jnp.float32) * (-2.0 * math.log(10000.0) / values.shape[-1])
    )
    angles = positions.astype(jnp.float32)[:, None] * frequency[None, :]
    cosine = jnp.cos(angles)[:, None, :]
    sine_part = jnp.sin(angles)[:, None, :]
    first_half = values[..., :half_dim]
    second_half = values[..., half_dim:]
    return jnp.concatenate(
        [
            first_half * cosine - second_half * sine_part,
            second_half * cosine + first_half * sine_part,
        ],
        axis=-1,
    )


def select_rows(chosen, source):
    one_hot = (
        chosen[:, None] == lax.broadcasted_iota(jnp.int32, (chosen.shape[0], source.shape[0]), 1)
    ).astype(source.dtype)
    return jnp.dot(one_hot, source, preferred_element_type=jnp.float32).astype(source.dtype)


def local(hidden, keep_first, keep_second, norm_gain, w_query, w_keyval):
    my_index = lax.axis_index("seq")
    odd = my_index % 2
    row_count = keep_second.shape[0]
    kept = keep_first.shape[1]
    query_cols = w_query.shape[1]
    kv_cols = w_keyval.shape[2]
    q_all, kv_all = all_weights(w_query, w_keyval.reshape(-1, 2 * kv_cols))

    other_picks = from_partner(keep_second, "seq", 0)
    own_kept = select_rows(keep_first[0], hidden)
    own_part = select_rows(keep_second - odd * kept, own_kept)
    other_part = select_rows(other_picks - odd * kept, own_kept)
    quarter = own_part + from_partner(other_part, "seq", 0)
    gathered = lax.all_gather(quarter, "tp", axis=1, tiled=True)
    widened = gathered.astype(jnp.float32)
    inv_rms = lax.rsqrt(jnp.mean(widened * widened, axis=1, keepdims=True) + eps)
    normed = (widened * inv_rms * norm_gain[None, :]).astype(jnp.bfloat16)
    query = jnp.dot(normed, q_all.reshape(-1, query_cols), preferred_element_type=jnp.float32)
    keyval = jnp.dot(normed, kv_all.reshape(-1, 2 * kv_cols), preferred_element_type=jnp.float32)
    query_heads = query_cols // HD
    kv_heads = kv_cols // HD
    positions = my_index % 4 * row_count + jnp.arange(row_count, dtype=jnp.int32)
    rot_query = rotate(query.reshape(row_count, query_heads, HD), positions).astype(jnp.bfloat16)
    keyval = keyval.reshape(row_count, 2, kv_heads, HD)
    rot_keys = rotate(keyval[:, 0], positions).astype(jnp.bfloat16)
    values = keyval[:, 1].astype(jnp.bfloat16)
    stacked = jnp.stack([rot_keys, values], axis=1)
    for bit_number in range(2):
        partner_keys = from_partner(stacked, "seq", bit_number)
        lower_half = my_index // (1 << bit_number) % 2 == 0
        stacked = jnp.where(
            lower_half,
            jnp.concatenate([stacked, partner_keys], axis=0),
            jnp.concatenate([partner_keys, stacked], axis=0),
        )
    group_size = query_heads // kv_heads
    grouped = rot_query.reshape(row_count, kv_heads, group_size, HD)
    scores = jnp.einsum(
        "qkgd,ckd->kgqc", grouped, stacked[:, 0], preferred_element_type=jnp.float32
    ) / math.sqrt(HD)
    causal = positions[:, None] >= jnp.arange(stacked.shape[0], dtype=jnp.int32)[None, :]
    scores = jnp.where(causal, scores, -jnp.inf)
    row_max = jnp.max(scores, axis=-1, keepdims=True)
    weights = jnp.exp(scores - row_max)
    weights = (weights / jnp.sum(weights, axis=-1, keepdims=True)).astype(jnp.bfloat16)
    result = jnp.einsum(
        "kgqc,ckd->qkgd", weights, stacked[:, 1], preferred_element_type=jnp.float32
    )
    return result.reshape(row_count, query_heads * HD).astype(jnp.bfloat16)


def solution(mesh):
    placed = (P("seq", "tp"), P("seq", None), P("seq"), P(), P("seq", "tp"), P("seq", None, "tp"))
    return jax.shard_map(
        local, mesh=mesh, in_specs=placed, out_specs=P("seq", "tp"), check_vma=False
    )
```

```python
import functools
import math

import jax
import jax.numpy as jnp
import numpy as np
from jax import lax
from jax.experimental import pallas as pl
from jax.experimental.pallas import tpu as pltpu
from jax.sharding import PartitionSpec as P

HD = 128
NX, NY, NZ = 4, 8, 4
LINE = 4
NT = 2 * NZ
MESH = pl.DeviceIdType.MESH
X_RIGHT, X_LEFT, Y_RIGHT, Y_LEFT, Z_OTHER = (1, 0, 0), (-1, 0, 0), (0, 1, 0), (0, -1, 0), (0, 0, 1)
COPIES = 97
BF16, F32 = jnp.bfloat16, jnp.float32

eps = 1e-05


def one_hot(picks, first, count):
    n = picks.shape[1]
    down = jnp.transpose(jnp.broadcast_to(picks, (128, n))) - first
    lane = lax.broadcasted_iota(jnp.int32, (n, 128), 1)
    return jnp.concatenate(
        [jnp.where(down == lane + start, 1.0, 0.0).astype(BF16) for start in range(0, count, 128)], axis=1
    )


def turned(values, cosine, sine):
    return values * cosine + pltpu.roll(values, HD // 2, 1) * sine


def kernel(
    hidden_ref, keep_ref, picks_ref, gain_ref, wq_ref, wkv_ref, angles_ref, out_ref,
    q_all, kv_all, hidden, kept, others, outgoing, incoming, rows_all, normed, angles, q_sum, span_kv,
    send_sems, recv_sems, local_sems,
):
    me = lax.axis_index("seq")
    tp = lax.axis_index("tp")
    zl, x, y = me // (NX * NY), me // NY % NX, me % NY
    zh, core = tp // 2, tp % 2
    odd = me % 2
    spot = me % LINE
    rows = picks_ref.shape[1]
    half = rows // 2
    features = hidden_ref.shape[1]
    choices = keep_ref.shape[1]

    def device(way):
        dx, dy, dz = way
        nx, ny, nz = lax.rem(x + dx + NX, NX), lax.rem(y + dy + NY, NY), lax.rem(zl + dz, 2)
        return (nz * (NX * NY) + nx * NY + ny, tp)

    def slot(dz, other):
        return lax.rem(zh + dz + NZ, NZ) * 2 + (1 - core if other else core)

    mate = (me + 1 - 2 * odd, tp)
    sibling = (me, tp + 1 - 2 * core)
    above, below = (me, slot(1, False)), (me, slot(-1, False))
    line = [
        lax.rem(spot // 2 * 2 + 1 - spot % 2, LINE),
        lax.rem(spot + 2, LINE),
        LINE - 1 - spot,
    ]

    def at(ref, other, xo, yo):
        plane = lax.rem(zl + other, 2)
        row = lax.rem(y + yo + 2 * NY, NY)
        if xo is None:
            return ref.at[plane, :, row]
        return ref.at[plane, lax.rem(x + xo + 2 * NX, NX), row]

    loads = [
        pltpu.make_async_copy(hidden_ref, hidden, local_sems.at[0]),
        pltpu.make_async_copy(wq_ref, at(q_all, 0, 0, 0), local_sems.at[1]),
        pltpu.make_async_copy(wkv_ref, at(kv_all, 0, 0, 0), local_sems.at[2]),
        pltpu.make_async_copy(angles_ref.at[:, pl.ds(pl.multiple_of(spot * rows, rows), rows)], angles, local_sems.at[3]),
    ]
    for load in loads:
        load.start()

    barrier = pltpu.get_barrier_semaphore()
    partners = [device(way) for way in (X_RIGHT, X_LEFT, Y_RIGHT, Y_LEFT, Z_OTHER)]
    partners += [sibling, above, below] + [(me - spot + line[1], tp), (me - spot + line[2], tp)]
    for partner in partners:
        pl.semaphore_signal(barrier, inc=1, device_id=partner, device_id_type=MESH)
    pl.semaphore_wait(barrier, len(partners))

    copies = []
    table = {}

    def push(src, dst, landing, where):
        number = len(copies)
        copy = pltpu.make_async_remote_copy(
            src_ref=src, dst_ref=dst, send_sem=send_sems.at[number], recv_sem=recv_sems.at[number],
            device_id=where, device_id_type=MESH,
        )
        copy.start()
        copies.append(copy)
        return pltpu.make_async_remote_copy(
            src_ref=landing, dst_ref=landing, send_sem=send_sems.at[number], recv_sem=recv_sems.at[number],
            device_id=where, device_id_type=MESH,
        )

    def send(ref, way, other, xo, yo, src=None):
        dst = at(ref, other, xo, yo)
        dx, dy, dz = way
        there = (other + dz) % 2, None if xo is None else xo - dx, yo - dy
        table[(id(ref), way) + there] = push(dst if src is None else src, dst, at(ref, *there), device(way))

    def arrived(ref, way, other, xo, yo):
        table.pop((id(ref), way, other, xo, yo)).wait_recv()

    picks_in = push(picks_ref, others, others, mate)
    send(kv_all, Z_OTHER, 0, 0, 0, wkv_ref)
    send(q_all, Z_OTHER, 0, 0, 0, wq_ref)
    for way in (X_RIGHT, X_LEFT):
        send(kv_all, way, 0, 0, 0, wkv_ref)
    for way in (Y_RIGHT, Y_LEFT):
        send(q_all, way, 0, 0, 0, wq_ref)
    for way in (X_RIGHT, X_LEFT):
        send(q_all, way, 0, 0, 0, wq_ref)

    first_hot = one_hot(keep_ref[...], 0, hidden.shape[0])
    loads[0].wait()
    kept[...] = jnp.dot(first_hot, hidden[...], preferred_element_type=F32).astype(BF16)
    picks_in.wait_recv()
    outgoing[...] = jnp.dot(
        one_hot(others[...], odd * choices, choices), kept[...], preferred_element_type=F32
    ).astype(BF16)
    rows_in = push(outgoing, incoming, incoming, mate)

    arrived(kv_all, Z_OTHER, 1, 0, 0)
    for way in (X_RIGHT, X_LEFT):
        send(kv_all, way, 1, 0, 0)
    arrived(q_all, Z_OTHER, 1, 0, 0)
    for way in (Y_RIGHT, Y_LEFT):
        send(q_all, way, 1, 0, 0)
    for way in (X_RIGHT, X_LEFT):
        send(q_all, way, 1, 0, 0)
    own_rows = jnp.dot(
        one_hot(picks_ref[...], odd * choices, choices), kept[...], preferred_element_type=F32
    ).astype(BF16)
    rows_all[tp] = own_rows
    arrived(kv_all, X_RIGHT, 0, -1, 0)
    send(kv_all, X_RIGHT, 0, -1, 0)
    arrived(kv_all, X_LEFT, 1, 1, 0)
    send(kv_all, X_LEFT, 1, 1, 0)
    arrived(kv_all, X_LEFT, 0, 1, 0)
    arrived(kv_all, X_RIGHT, 1, -1, 0)
    loads[2].wait()

    def second_hop(yo):
        arrived(q_all, X_RIGHT, 0, -1, yo)
        send(q_all, X_RIGHT, 0, -1, yo)
        arrived(q_all, X_LEFT, 1, 1, yo)
        send(q_all, X_LEFT, 1, 1, yo)

    def kv_hop(step):
        if step == 0:
            arrived(kv_all, X_RIGHT, 0, -2, 0)
            arrived(kv_all, X_LEFT, 1, 2, 0)
            for way in (Y_RIGHT, Y_LEFT):
                for other in (0, 1):
                    send(kv_all, way, other, None, 0)
            return
        for other in (0, 1):
            for way, sign, far in ((Y_RIGHT, -1, 4 - other), (Y_LEFT, 1, 3 + other)):
                if step <= far:
                    arrived(kv_all, way, other, None, sign * step)
                    if step < far:
                        send(kv_all, way, other, None, sign * step)

    def q_hop(step):
        for other in (0, 1):
            for way, sign, far in ((Y_RIGHT, -1, 4 - other), (Y_LEFT, 1, 3 + other)):
                if step <= far:
                    arrived(q_all, way, other, 0, sign * step)
                    if step < far:
                        send(q_all, way, other, 0, sign * step)
                    for side in (X_RIGHT, X_LEFT):
                        send(q_all, side, other, 0, sign * step)

    def block(dz, other, part=None):
        ref = rows_all.at[slot(dz, other)]
        if part is None:
            return ref
        return ref.at[pl.ds(part * half, half)]

    q_hop(1)
    kv_hop(0)
    rows_in.wait_recv()
    rows_all[tp] = rows_all[tp] + incoming[...]
    mine = block(0, False)
    to_above = push(mine, mine, block(-1, False), above)
    to_below = push(mine, mine, block(1, False), below)
    crossed = [push(mine, mine, block(0, True), sibling)]
    second_hop(0)
    q_hop(2)
    second_hop(-1)
    second_hop(1)
    kv_hop(1)
    q_hop(3)
    second_hop(-2)
    to_above.wait_recv()
    far_above = push(block(-1, False, 0), block(-1, False, 0), block(2, False, 0), above)
    to_below.wait_recv()
    far_below = push(block(1, False, 1), block(1, False, 1), block(2, False, 1), below)
    crossed.append(push(block(-1, False), block(-1, False), block(-1, True), sibling))
    crossed.append(push(block(1, False), block(1, False), block(1, True), sibling))
    kv_hop(2)
    second_hop(2)
    for other, way, sign in ((0, Y_RIGHT, -1), (1, Y_LEFT, 1)):
        arrived(q_all, way, other, 0, sign * 4)
        for side in (X_RIGHT, X_LEFT):
            send(q_all, side, other, 0, sign * 4)
    second_hop(-3)
    far_above.wait_recv()
    far_below.wait_recv()
    crossed.append(push(block(2, False), block(2, False), block(2, True), sibling))
    kv_hop(3)
    second_hop(3)
    arrived(q_all, X_RIGHT, 0, -1, -4)
    send(q_all, X_RIGHT, 0, -1, -4)
    arrived(q_all, X_LEFT, 1, 1, 4)
    send(q_all, X_LEFT, 1, 1, 4)

    for copy in crossed:
        copy.wait_recv()
    squares = jnp.zeros((rows, 128), F32)
    for t in range(NT):
        wide = rows_all[t].astype(F32)
        wide = wide * wide
        for start in range(0, features, 128):
            squares = squares + wide[:, start:start + 128]
    inverse = lax.rsqrt(jnp.sum(squares, axis=1, keepdims=True) / (NT * features) + eps)
    for t in range(NT):
        normed[t] = (
            rows_all[t].astype(F32) * inverse * gain_ref[0:1, t * features:(t + 1) * features]
        ).astype(BF16)

    loads[3].wait()
    cosine, sine = angles[0], angles[1]
    kv_hop(4)
    kv_cols = kv_all.shape[-1]

    def kv_part(t, total):
        weights = kv_all[t // NX, t % NX].reshape(features, kv_cols)
        return total + jnp.dot(normed[t], weights, preferred_element_type=F32)

    keyval = lax.fori_loop(0, NT, kv_part, jnp.zeros((rows, kv_cols), F32))
    span_kv[spot] = jnp.concatenate(
        [turned(keyval[:, :HD], cosine, sine), keyval[:, HD:]], axis=1
    ).astype(BF16)
    shared = [
        push(span_kv.at[spot], span_kv.at[spot], span_kv.at[place], (me - spot + place, tp))
        for place in line
    ]

    loads[1].wait()
    q_sum[...] = jnp.zeros_like(q_sum)

    def q_part(yo):
        low = 1 if yo < -3 else 0
        for other in (0, 1):
            off = 4 if low and other else yo
            for way, xo in ((X_RIGHT, -1), (X_LEFT, 1), (X_RIGHT if other == 0 else X_LEFT, -2 if other == 0 else 2)):
                key = (id(q_all), way, other, xo, off)
                if key in table:
                    arrived(q_all, way, other, xo, off)
        row = lax.rem(y + yo + NY, NY)
        depth = q_all.shape[3]
        columns = pl.ds(pl.multiple_of(row * depth, depth), depth)

        def add(xx, carry):
            q_sum[...] += jnp.dot(
                normed[xx, :, columns], q_all[0, xx, row], preferred_element_type=F32
            ) + jnp.dot(normed[NX + xx, :, columns], q_all[1, xx, row], preferred_element_type=F32)
            return carry

        lax.fori_loop(0, NX, add, 0)

    for yo in (0, -1, 1, -2, 2, -3, 3, -4):
        q_part(yo)

    for copy in shared:
        copy.wait_recv()
    span = LINE * rows
    keys = span_kv[:, :, :HD].reshape(span, HD)
    values = span_kv[:, :, HD:].reshape(span, HD)
    position = lax.broadcasted_iota(jnp.int32, (rows, span), 0) + spot * rows
    causal = position >= lax.broadcasted_iota(jnp.int32, (rows, span), 1)
    factor = math.log2(math.e) / math.sqrt(HD)
    for head in range(q_sum.shape[1] // HD):
        lanes = slice(head * HD, (head + 1) * HD)
        rot_query = turned(q_sum[:, lanes], cosine, sine).astype(BF16)
        scores = lax.dot_general(rot_query, keys, (((1,), (1,)), ((), ())), preferred_element_type=F32)
        scores = jnp.where(causal, scores, -jnp.inf)
        weights = jnp.exp2((scores - jnp.max(scores, axis=1, keepdims=True)) * factor)
        weights = (weights * (1.0 / jnp.sum(weights, axis=1, keepdims=True))).astype(BF16)
        out_ref[:, lanes] = jnp.dot(weights, values, preferred_element_type=F32).astype(BF16)

    assert not table
    for copy in copies:
        copy.wait_send()


def local(angles, hidden, keep_first, keep_second, norm_gain, w_query, w_keyval):
    rows = keep_second.shape[0]
    depth, q_cols = w_query.shape
    kv_cols = 2 * w_keyval.shape[2]
    span, features = hidden.shape
    choices = keep_first.shape[1]
    vmem = pl.BlockSpec(memory_space=pltpu.VMEM)
    away = pl.BlockSpec(memory_space=pl.ANY)
    return pl.pallas_call(
        kernel,
        out_shape=jax.ShapeDtypeStruct((rows, q_cols), BF16),
        in_specs=[away, vmem, vmem, vmem, away, away, away],
        out_specs=vmem,
        scratch_shapes=[
            pltpu.VMEM((2, NX, NY, depth, q_cols), BF16),
            pltpu.VMEM((2, NX, NY, depth, kv_cols), BF16),
            pltpu.VMEM((span, features), BF16),
            pltpu.VMEM((choices, features), BF16),
            pltpu.VMEM((1, rows), jnp.int32),
            pltpu.VMEM((rows, features), BF16),
            pltpu.VMEM((rows, features), BF16),
            pltpu.VMEM((NT, rows, features), BF16),
            pltpu.VMEM((NT, rows, features), BF16),
            pltpu.VMEM((2, rows, HD), F32),
            pltpu.VMEM((rows, q_cols), F32),
            pltpu.VMEM((LINE, rows, kv_cols), BF16),
            pltpu.SemaphoreType.DMA((COPIES,)),
            pltpu.SemaphoreType.DMA((COPIES,)),
            pltpu.SemaphoreType.DMA((4,)),
        ],
        compiler_params=pltpu.CompilerParams(
            collective_id=0, has_side_effects=True, vmem_limit_bytes=56 * 1024 * 1024
        ),
        cost_estimate=pl.CostEstimate(flops=7_000_000_000, bytes_accessed=20_000_000, transcendentals=1_000_000),
    )(
        hidden, keep_first, keep_second.reshape(1, rows), norm_gain.reshape(1, -1), w_query,
        w_keyval.reshape(depth, kv_cols), angles,
    )


def rotary_tables(length):
    spread = np.exp(np.arange(HD // 2, dtype=np.float32) * np.float32(-2.0 * math.log(10000.0) / HD))
    turn = np.arange(length, dtype=np.float32)[:, None] * spread.astype(np.float32)[None, :]
    cosine, sine = np.cos(turn.astype(np.float64)), np.sin(turn.astype(np.float64))
    return np.stack(
        [np.concatenate([cosine, cosine], axis=1), np.concatenate([-sine, sine], axis=1)]
    ).astype(np.float32)


def solution(mesh):
    placed = (P("seq", "tp"), P("seq", None), P("seq"), P(), P("seq", "tp"), P("seq", None, "tp"))
    tables = rotary_tables(1024)

    def run(*args):
        return jax.shard_map(
            local, mesh=mesh, in_specs=(P(),) + placed, out_specs=P("seq", "tp"), check_vma=False
        )(jnp.asarray(tables), *args)

    return run
```

```python
import functools
import math

import jax
import jax.numpy as jnp
import numpy as np
from jax import lax
from jax.experimental import pallas as pl
from jax.experimental.pallas import tpu as pltpu
from jax.sharding import PartitionSpec as P

HD = 128
NX, NY, NZ = 4, 8, 4
LINE = 4
NT = 2 * NZ
MESH = pl.DeviceIdType.MESH
X_RIGHT, X_LEFT, Y_RIGHT, Y_LEFT, Z_OTHER = (1, 0, 0), (-1, 0, 0), (0, 1, 0), (0, -1, 0), (0, 0, 1)
COPIES = 97
BF16, F32 = jnp.bfloat16, jnp.float32

eps = 1e-05


def one_hot(picks, first, count):
    n = picks.shape[1]
    down = jnp.transpose(jnp.broadcast_to(picks, (128, n))) - first
    lane = lax.broadcasted_iota(jnp.int32, (n, 128), 1)
    return jnp.concatenate(
        [jnp.where(down == lane + start, 1.0, 0.0).astype(BF16) for start in range(0, count, 128)], axis=1
    )


def turned(values, cosine, sine):
    return values * cosine + pltpu.roll(values, HD // 2, 1) * sine


def kernel(
    hidden_ref, keep_ref, picks_ref, gain_ref, wq_ref, wkv_in, angles_ref, out_ref,
    wkv_ref, q_all, kv_all, hidden, kept, others, outgoing, incoming, rows_all, normed, angles, q_sum, span_kv,
    send_sems, recv_sems, local_sems,
):
    me = lax.axis_index("seq")
    tp = lax.axis_index("tp")
    zl, x, y = me // (NX * NY), me // NY % NX, me % NY
    zh, core = tp // 2, tp % 2
    odd = me % 2
    spot = me % LINE
    rows = picks_ref.shape[1]
    half = rows // 2
    features = hidden_ref.shape[1]
    choices = keep_ref.shape[1]

    def device(way):
        dx, dy, dz = way
        nx, ny, nz = lax.rem(x + dx + NX, NX), lax.rem(y + dy + NY, NY), lax.rem(zl + dz, 2)
        return (nz * (NX * NY) + nx * NY + ny, tp)

    def slot(dz, other):
        return lax.rem(zh + dz + NZ, NZ) * 2 + (1 - core if other else core)

    mate = (me + 1 - 2 * odd, tp)
    sibling = (me, tp + 1 - 2 * core)
    above, below = (me, slot(1, False)), (me, slot(-1, False))
    line = [
        lax.rem(spot // 2 * 2 + 1 - spot % 2, LINE),
        lax.rem(spot + 2, LINE),
        LINE - 1 - spot,
    ]

    def at(ref, other, xo, yo):
        plane = lax.rem(zl + other, 2)
        row = lax.rem(y + yo + 2 * NY, NY)
        if xo is None:
            return ref.at[plane, :, row]
        return ref.at[plane, lax.rem(x + xo + 2 * NX, NX), row]

    wkv_ref[...] = jnp.concatenate([wkv_in[:, 0, :], wkv_in[:, 1, :]], axis=1)
    loads = [
        pltpu.make_async_copy(hidden_ref, hidden, local_sems.at[0]),
        pltpu.make_async_copy(wq_ref, at(q_all, 0, 0, 0), local_sems.at[1]),
        pltpu.make_async_copy(wkv_ref, at(kv_all, 0, 0, 0), local_sems.at[2]),
        pltpu.make_async_copy(angles_ref.at[:, pl.ds(pl.multiple_of(spot * rows, rows), rows)], angles, local_sems.at[3]),
    ]
    for load in loads:
        load.start()

    barrier = pltpu.get_barrier_semaphore()
    partners = [device(way) for way in (X_RIGHT, X_LEFT, Y_RIGHT, Y_LEFT, Z_OTHER)]
    partners += [sibling, above, below] + [(me - spot + line[1], tp), (me - spot + line[2], tp)]
    for partner in partners:
        pl.semaphore_signal(barrier, inc=1, device_id=partner, device_id_type=MESH)
    pl.semaphore_wait(barrier, len(partners))

    copies = []
    table = {}

    def push(src, dst, landing, where):
        number = len(copies)
        copy = pltpu.make_async_remote_copy(
            src_ref=src, dst_ref=dst, send_sem=send_sems.at[number], recv_sem=recv_sems.at[number],
            device_id=where, device_id_type=MESH,
        )
        copy.start()
        copies.append(copy)
        return pltpu.make_async_remote_copy(
            src_ref=landing, dst_ref=landing, send_sem=send_sems.at[number], recv_sem=recv_sems.at[number],
            device_id=where, device_id_type=MESH,
        )

    def send(ref, way, other, xo, yo, src=None):
        dst = at(ref, other, xo, yo)
        dx, dy, dz = way
        there = (other + dz) % 2, None if xo is None else xo - dx, yo - dy
        table[(id(ref), way) + there] = push(dst if src is None else src, dst, at(ref, *there), device(way))

    def arrived(ref, way, other, xo, yo):
        table.pop((id(ref), way, other, xo, yo)).wait_recv()

    picks_in = push(picks_ref, others, others, mate)
    send(kv_all, Z_OTHER, 0, 0, 0, wkv_ref)
    send(q_all, Z_OTHER, 0, 0, 0, wq_ref)
    for way in (X_RIGHT, X_LEFT):
        send(kv_all, way, 0, 0, 0, wkv_ref)
    for way in (Y_RIGHT, Y_LEFT):
        send(q_all, way, 0, 0, 0, wq_ref)
    for way in (X_RIGHT, X_LEFT):
        send(q_all, way, 0, 0, 0, wq_ref)

    first_hot = one_hot(keep_ref[...], 0, hidden.shape[0])
    loads[0].wait()
    kept[...] = jnp.dot(first_hot, hidden[...], preferred_element_type=F32).astype(BF16)
    picks_in.wait_recv()
    outgoing[...] = jnp.dot(
        one_hot(others[...], odd * choices, choices), kept[...], preferred_element_type=F32
    ).astype(BF16)
    rows_in = push(outgoing, incoming, incoming, mate)

    arrived(kv_all, Z_OTHER, 1, 0, 0)
    for way in (X_RIGHT, X_LEFT):
        send(kv_all, way, 1, 0, 0)
    arrived(q_all, Z_OTHER, 1, 0, 0)
    for way in (Y_RIGHT, Y_LEFT):
        send(q_all, way, 1, 0, 0)
    for way in (X_RIGHT, X_LEFT):
        send(q_all, way, 1, 0, 0)
    own_rows = jnp.dot(
        one_hot(picks_ref[...], odd * choices, choices), kept[...], preferred_element_type=F32
    ).astype(BF16)
    rows_all[tp] = own_rows
    arrived(kv_all, X_RIGHT, 0, -1, 0)
    send(kv_all, X_RIGHT, 0, -1, 0)
    arrived(kv_all, X_LEFT, 1, 1, 0)
    send(kv_all, X_LEFT, 1, 1, 0)
    arrived(kv_all, X_LEFT, 0, 1, 0)
    arrived(kv_all, X_RIGHT, 1, -1, 0)
    loads[2].wait()

    def second_hop(yo):
        arrived(q_all, X_RIGHT, 0, -1, yo)
        send(q_all, X_RIGHT, 0, -1, yo)
        arrived(q_all, X_LEFT, 1, 1, yo)
        send(q_all, X_LEFT, 1, 1, yo)

    def kv_hop(step):
        if step == 0:
            arrived(kv_all, X_RIGHT, 0, -2, 0)
            arrived(kv_all, X_LEFT, 1, 2, 0)
            for way in (Y_RIGHT, Y_LEFT):
                for other in (0, 1):
                    send(kv_all, way, other, None, 0)
            return
        for other in (0, 1):
            for way, sign, far in ((Y_RIGHT, -1, 4 - other), (Y_LEFT, 1, 3 + other)):
                if step <= far:
                    arrived(kv_all, way, other, None, sign * step)
                    if step < far:
                        send(kv_all, way, other, None, sign * step)

    def q_hop(step):
        for other in (0, 1):
            for way, sign, far in ((Y_RIGHT, -1, 4 - other), (Y_LEFT, 1, 3 + other)):
                if step <= far:
                    arrived(q_all, way, other, 0, sign * step)
                    if step < far:
                        send(q_all, way, other, 0, sign * step)
                    for side in (X_RIGHT, X_LEFT):
                        send(q_all, side, other, 0, sign * step)

    def block(dz, other, part=None):
        ref = rows_all.at[slot(dz, other)]
        if part is None:
            return ref
        return ref.at[pl.ds(part * half, half)]

    q_hop(1)
    kv_hop(0)
    rows_in.wait_recv()
    rows_all[tp] = rows_all[tp] + incoming[...]
    mine = block(0, False)
    to_above = push(mine, mine, block(-1, False), above)
    to_below = push(mine, mine, block(1, False), below)
    crossed = [push(mine, mine, block(0, True), sibling)]
    second_hop(0)
    q_hop(2)
    second_hop(-1)
    second_hop(1)
    kv_hop(1)
    q_hop(3)
    second_hop(-2)
    to_above.wait_recv()
    far_above = push(block(-1, False, 0), block(-1, False, 0), block(2, False, 0), above)
    to_below.wait_recv()
    far_below = push(block(1, False, 1), block(1, False, 1), block(2, False, 1), below)
    crossed.append(push(block(-1, False), block(-1, False), block(-1, True), sibling))
    crossed.append(push(block(1, False), block(1, False), block(1, True), sibling))
    kv_hop(2)
    second_hop(2)
    for other, way, sign in ((0, Y_RIGHT, -1), (1, Y_LEFT, 1)):
        arrived(q_all, way, other, 0, sign * 4)
        for side in (X_RIGHT, X_LEFT):
            send(q_all, side, other, 0, sign * 4)
    second_hop(-3)
    far_above.wait_recv()
    far_below.wait_recv()
    crossed.append(push(block(2, False), block(2, False), block(2, True), sibling))
    kv_hop(3)
    second_hop(3)
    arrived(q_all, X_RIGHT, 0, -1, -4)
    send(q_all, X_RIGHT, 0, -1, -4)
    arrived(q_all, X_LEFT, 1, 1, 4)
    send(q_all, X_LEFT, 1, 1, 4)

    for copy in crossed:
        copy.wait_recv()
    squares = jnp.zeros((rows, 128), F32)
    for t in range(NT):
        wide = rows_all[t].astype(F32)
        wide = wide * wide
        for start in range(0, features, 128):
            squares = squares + wide[:, start:start + 128]
    inverse = lax.rsqrt(jnp.sum(squares, axis=1, keepdims=True) / (NT * features) + eps)
    for t in range(NT):
        normed[t] = (
            rows_all[t].astype(F32) * inverse * gain_ref[0:1, t * features:(t + 1) * features]
        ).astype(BF16)

    loads[3].wait()
    cosine, sine = angles[0], angles[1]
    kv_hop(4)
    kv_cols = kv_all.shape[-1]

    def kv_part(t, total):
        weights = kv_all[t // NX, t % NX].reshape(features, kv_cols)
        return total + jnp.dot(normed[t], weights, preferred_element_type=F32)

    keyval = lax.fori_loop(0, NT, kv_part, jnp.zeros((rows, kv_cols), F32))
    span_kv[spot] = jnp.concatenate(
        [turned(keyval[:, :HD], cosine, sine), keyval[:, HD:]], axis=1
    ).astype(BF16)
    shared = [
        push(span_kv.at[spot], span_kv.at[spot], span_kv.at[place], (me - spot + place, tp))
        for place in line
    ]

    loads[1].wait()
    q_sum[...] = jnp.zeros_like(q_sum)

    def q_part(yo):
        low = 1 if yo < -3 else 0
        for other in (0, 1):
            off = 4 if low and other else yo
            for way, xo in ((X_RIGHT, -1), (X_LEFT, 1), (X_RIGHT if other == 0 else X_LEFT, -2 if other == 0 else 2)):
                key = (id(q_all), way, other, xo, off)
                if key in table:
                    arrived(q_all, way, other, xo, off)
        row = lax.rem(y + yo + NY, NY)
        depth = q_all.shape[3]
        columns = pl.ds(pl.multiple_of(row * depth, depth), depth)

        def add(xx, carry):
            q_sum[...] += jnp.dot(
                normed[xx, :, columns], q_all[0, xx, row], preferred_element_type=F32
            ) + jnp.dot(normed[NX + xx, :, columns], q_all[1, xx, row], preferred_element_type=F32)
            return carry

        lax.fori_loop(0, NX, add, 0)

    for yo in (0, -1, 1, -2, 2, -3, 3, -4):
        q_part(yo)

    for copy in shared:
        copy.wait_recv()
    span = LINE * rows
    keys = span_kv[:, :, :HD].reshape(span, HD)
    values = span_kv[:, :, HD:].reshape(span, HD)
    position = lax.broadcasted_iota(jnp.int32, (rows, span), 0) + spot * rows
    causal = position >= lax.broadcasted_iota(jnp.int32, (rows, span), 1)
    factor = math.log2(math.e) / math.sqrt(HD)
    for head in range(q_sum.shape[1] // HD):
        lanes = slice(head * HD, (head + 1) * HD)
        rot_query = turned(q_sum[:, lanes], cosine, sine).astype(BF16)
        scores = lax.dot_general(rot_query, keys, (((1,), (1,)), ((), ())), preferred_element_type=F32)
        scores = jnp.where(causal, scores, -jnp.inf)
        weights = jnp.exp2((scores - jnp.max(scores, axis=1, keepdims=True)) * factor)
        weights = (weights * (1.0 / jnp.sum(weights, axis=1, keepdims=True))).astype(BF16)
        out_ref[:, lanes] = jnp.dot(weights, values, preferred_element_type=F32).astype(BF16)

    assert not table
    for copy in copies:
        copy.wait_send()


def local(angles, hidden, keep_first, keep_second, norm_gain, w_query, w_keyval):
    rows = keep_second.shape[0]
    depth, q_cols = w_query.shape
    kv_cols = 2 * w_keyval.shape[2]
    span, features = hidden.shape
    choices = keep_first.shape[1]
    vmem = pl.BlockSpec(memory_space=pltpu.VMEM)
    away = pl.BlockSpec(memory_space=pl.ANY)
    return pl.pallas_call(
        kernel,
        out_shape=jax.ShapeDtypeStruct((rows, q_cols), BF16),
        in_specs=[away, vmem, vmem, vmem, away, vmem, away],
        out_specs=vmem,
        scratch_shapes=[
            pltpu.VMEM((depth, kv_cols), BF16),
            pltpu.VMEM((2, NX, NY, depth, q_cols), BF16),
            pltpu.VMEM((2, NX, NY, depth, kv_cols), BF16),
            pltpu.VMEM((span, features), BF16),
            pltpu.VMEM((choices, features), BF16),
            pltpu.VMEM((1, rows), jnp.int32),
            pltpu.VMEM((rows, features), BF16),
            pltpu.VMEM((rows, features), BF16),
            pltpu.VMEM((NT, rows, features), BF16),
            pltpu.VMEM((NT, rows, features), BF16),
            pltpu.VMEM((2, rows, HD), F32),
            pltpu.VMEM((rows, q_cols), F32),
            pltpu.VMEM((LINE, rows, kv_cols), BF16),
            pltpu.SemaphoreType.DMA((COPIES,)),
            pltpu.SemaphoreType.DMA((COPIES,)),
            pltpu.SemaphoreType.DMA((4,)),
        ],
        compiler_params=pltpu.CompilerParams(
            collective_id=0, has_side_effects=True, vmem_limit_bytes=56 * 1024 * 1024
        ),
        cost_estimate=pl.CostEstimate(flops=7_000_000_000, bytes_accessed=20_000_000, transcendentals=1_000_000),
    )(
        hidden, keep_first, keep_second.reshape(1, rows), norm_gain.reshape(1, -1), w_query,
        w_keyval, angles,
    )


def rotary_tables(length):
    spread = np.exp(np.arange(HD // 2, dtype=np.float32) * np.float32(-2.0 * math.log(10000.0) / HD))
    turn = np.arange(length, dtype=np.float32)[:, None] * spread.astype(np.float32)[None, :]
    cosine, sine = np.cos(turn.astype(np.float64)), np.sin(turn.astype(np.float64))
    return np.stack(
        [np.concatenate([cosine, cosine], axis=1), np.concatenate([-sine, sine], axis=1)]
    ).astype(np.float32)


def solution(mesh):
    placed = (P("seq", "tp"), P("seq", None), P("seq"), P(), P("seq", "tp"), P("seq", None, "tp"))
    tables = rotary_tables(1024)

    def run(*args):
        return jax.shard_map(
            local, mesh=mesh, in_specs=(P(),) + placed, out_specs=P("seq", "tp"), check_vma=False
        )(jnp.asarray(tables), *args)

    return run
```

```python
import functools
import math

import jax
import jax.numpy as jnp
import numpy as np
from jax import lax
from jax.experimental import pallas as pl
from jax.experimental.pallas import tpu as pltpu
from jax.sharding import PartitionSpec as P

HD = 128
NX, NY, NZ = 4, 8, 4
LINE = 4
NT = 2 * NZ
MESH = pl.DeviceIdType.MESH
X_RIGHT, X_LEFT, Y_RIGHT, Y_LEFT, Z_OTHER = (1, 0, 0), (-1, 0, 0), (0, 1, 0), (0, -1, 0), (0, 0, 1)
COPIES = 97
BF16, F32 = jnp.bfloat16, jnp.float32

eps = 1e-05


def one_hot(picks, first, count):
    n = picks.shape[1]
    down = jnp.transpose(jnp.broadcast_to(picks, (128, n))) - first
    lane = lax.broadcasted_iota(jnp.int32, (n, 128), 1)
    return jnp.concatenate(
        [jnp.where(down == lane + start, 1.0, 0.0).astype(BF16) for start in range(0, count, 128)], axis=1
    )


def turned(values, cosine, sine):
    return values * cosine + pltpu.roll(values, HD // 2, 1) * sine


def kernel(
    hidden_ref, keep_ref, picks_ref, gain_ref, wq_ref, wkv_in, angles_ref, out_ref,
    wkv_ref, q_all, kv_all, hidden, kept, others, outgoing, incoming, rows_all, normed, angles, q_sum, early, span_kv,
    send_sems, recv_sems, local_sems,
):
    me = lax.axis_index("seq")
    tp = lax.axis_index("tp")
    zl, x, y = me // (NX * NY), me // NY % NX, me % NY
    zh, core = tp // 2, tp % 2
    odd = me % 2
    spot = me % LINE
    rows = picks_ref.shape[1]
    half = rows // 2
    features = hidden_ref.shape[1]
    choices = keep_ref.shape[1]

    def device(way):
        dx, dy, dz = way
        nx, ny, nz = lax.rem(x + dx + NX, NX), lax.rem(y + dy + NY, NY), lax.rem(zl + dz, 2)
        return (nz * (NX * NY) + nx * NY + ny, tp)

    def slot(dz, other):
        return lax.rem(zh + dz + NZ, NZ) * 2 + (1 - core if other else core)

    mate = (me + 1 - 2 * odd, tp)
    sibling = (me, tp + 1 - 2 * core)
    above, below = (me, slot(1, False)), (me, slot(-1, False))
    line = [
        lax.rem(spot // 2 * 2 + 1 - spot % 2, LINE),
        lax.rem(spot + 2, LINE),
        LINE - 1 - spot,
    ]

    def at(ref, other, xo, yo):
        plane = lax.rem(zl + other, 2)
        row = lax.rem(y + yo + 2 * NY, NY)
        if xo is None:
            return ref.at[plane, :, row]
        return ref.at[plane, lax.rem(x + xo + 2 * NX, NX), row]

    wkv_ref[...] = jnp.concatenate([wkv_in[:, 0, :], wkv_in[:, 1, :]], axis=1)
    loads = [
        pltpu.make_async_copy(hidden_ref, hidden, local_sems.at[0]),
        pltpu.make_async_copy(wq_ref, at(q_all, 0, 0, 0), local_sems.at[1]),
        pltpu.make_async_copy(wkv_ref, at(kv_all, 0, 0, 0), local_sems.at[2]),
        pltpu.make_async_copy(angles_ref.at[:, pl.ds(pl.multiple_of(spot * rows, rows), rows)], angles, local_sems.at[3]),
    ]
    for load in loads:
        load.start()

    barrier = pltpu.get_barrier_semaphore()
    partners = [device(way) for way in (X_RIGHT, X_LEFT, Y_RIGHT, Y_LEFT, Z_OTHER)]
    partners += [sibling, above, below] + [(me - spot + line[1], tp), (me - spot + line[2], tp)]
    for partner in partners:
        pl.semaphore_signal(barrier, inc=1, device_id=partner, device_id_type=MESH)
    pl.semaphore_wait(barrier, len(partners))

    copies = []
    table = {}

    def push(src, dst, landing, where):
        number = len(copies)
        copy = pltpu.make_async_remote_copy(
            src_ref=src, dst_ref=dst, send_sem=send_sems.at[number], recv_sem=recv_sems.at[number],
            device_id=where, device_id_type=MESH,
        )
        copy.start()
        copies.append(copy)
        return pltpu.make_async_remote_copy(
            src_ref=landing, dst_ref=landing, send_sem=send_sems.at[number], recv_sem=recv_sems.at[number],
            device_id=where, device_id_type=MESH,
        )

    def send(ref, way, other, xo, yo, src=None):
        dst = at(ref, other, xo, yo)
        dx, dy, dz = way
        there = (other + dz) % 2, None if xo is None else xo - dx, yo - dy
        table[(id(ref), way) + there] = push(dst if src is None else src, dst, at(ref, *there), device(way))

    def arrived(ref, way, other, xo, yo):
        table.pop((id(ref), way, other, xo, yo)).wait_recv()

    picks_in = push(picks_ref, others, others, mate)
    send(kv_all, Z_OTHER, 0, 0, 0, wkv_ref)
    send(q_all, Z_OTHER, 0, 0, 0, wq_ref)
    for way in (X_RIGHT, X_LEFT):
        send(kv_all, way, 0, 0, 0, wkv_ref)
    for way in (Y_RIGHT, Y_LEFT):
        send(q_all, way, 0, 0, 0, wq_ref)
    for way in (X_RIGHT, X_LEFT):
        send(q_all, way, 0, 0, 0, wq_ref)

    first_hot = one_hot(keep_ref[...], 0, hidden.shape[0])
    loads[0].wait()
    kept[...] = jnp.dot(first_hot, hidden[...], preferred_element_type=F32).astype(BF16)
    picks_in.wait_recv()
    outgoing[...] = jnp.dot(
        one_hot(others[...], odd * choices, choices), kept[...], preferred_element_type=F32
    ).astype(BF16)
    rows_in = push(outgoing, incoming, incoming, mate)

    arrived(kv_all, Z_OTHER, 1, 0, 0)
    for way in (X_RIGHT, X_LEFT):
        send(kv_all, way, 1, 0, 0)
    arrived(q_all, Z_OTHER, 1, 0, 0)
    for way in (Y_RIGHT, Y_LEFT):
        send(q_all, way, 1, 0, 0)
    for way in (X_RIGHT, X_LEFT):
        send(q_all, way, 1, 0, 0)
    own_rows = jnp.dot(
        one_hot(picks_ref[...], odd * choices, choices), kept[...], preferred_element_type=F32
    ).astype(BF16)
    rows_all[tp] = own_rows
    arrived(kv_all, X_RIGHT, 0, -1, 0)
    send(kv_all, X_RIGHT, 0, -1, 0)
    arrived(kv_all, X_LEFT, 1, 1, 0)
    send(kv_all, X_LEFT, 1, 1, 0)
    arrived(kv_all, X_LEFT, 0, 1, 0)
    arrived(kv_all, X_RIGHT, 1, -1, 0)
    loads[2].wait()

    def second_hop(yo):
        arrived(q_all, X_RIGHT, 0, -1, yo)
        send(q_all, X_RIGHT, 0, -1, yo)
        arrived(q_all, X_LEFT, 1, 1, yo)
        send(q_all, X_LEFT, 1, 1, yo)

    def kv_hop(step):
        if step == 0:
            arrived(kv_all, X_RIGHT, 0, -2, 0)
            arrived(kv_all, X_LEFT, 1, 2, 0)
            for way in (Y_RIGHT, Y_LEFT):
                for other in (0, 1):
                    send(kv_all, way, other, None, 0)
            return
        for other in (0, 1):
            for way, sign, far in ((Y_RIGHT, -1, 4 - other), (Y_LEFT, 1, 3 + other)):
                if step <= far:
                    arrived(kv_all, way, other, None, sign * step)
                    if step < far:
                        send(kv_all, way, other, None, sign * step)

    def q_hop(step):
        for other in (0, 1):
            for way, sign, far in ((Y_RIGHT, -1, 4 - other), (Y_LEFT, 1, 3 + other)):
                if step <= far:
                    arrived(q_all, way, other, 0, sign * step)
                    if step < far:
                        send(q_all, way, other, 0, sign * step)
                    for side in (X_RIGHT, X_LEFT):
                        send(q_all, side, other, 0, sign * step)

    def block(dz, other, part=None):
        ref = rows_all.at[slot(dz, other)]
        if part is None:
            return ref
        return ref.at[pl.ds(part * half, half)]

    q_hop(1)
    kv_hop(0)
    rows_in.wait_recv()
    rows_all[tp] = rows_all[tp] + incoming[...]
    mine = block(0, False)
    to_above = push(mine, mine, block(-1, False), above)
    to_below = push(mine, mine, block(1, False), below)
    crossed = [push(mine, mine, block(0, True), sibling)]
    second_hop(0)
    q_hop(2)
    second_hop(-1)
    second_hop(1)
    kv_hop(1)
    q_hop(3)
    second_hop(-2)
    to_above.wait_recv()
    far_above = push(block(-1, False, 0), block(-1, False, 0), block(2, False, 0), above)
    to_below.wait_recv()
    far_below = push(block(1, False, 1), block(1, False, 1), block(2, False, 1), below)
    crossed.append(push(block(-1, False), block(-1, False), block(-1, True), sibling))
    crossed.append(push(block(1, False), block(1, False), block(1, True), sibling))
    kv_hop(2)
    second_hop(2)
    for other, way, sign in ((0, Y_RIGHT, -1), (1, Y_LEFT, 1)):
        arrived(q_all, way, other, 0, sign * 4)
        for side in (X_RIGHT, X_LEFT):
            send(q_all, side, other, 0, sign * 4)
    second_hop(-3)
    far_above.wait_recv()
    far_below.wait_recv()
    crossed.append(push(block(2, False), block(2, False), block(2, True), sibling))
    kv_hop(3)
    second_hop(3)
    arrived(q_all, X_RIGHT, 0, -1, -4)
    send(q_all, X_RIGHT, 0, -1, -4)
    arrived(q_all, X_LEFT, 1, 1, 4)
    send(q_all, X_LEFT, 1, 1, 4)

    for copy in crossed:
        copy.wait_recv()
    squares = jnp.zeros((rows, 128), F32)
    for t in range(NT):
        wide = rows_all[t].astype(F32)
        wide = wide * wide
        for start in range(0, features, 128):
            squares = squares + wide[:, start:start + 128]
    inverse = lax.rsqrt(jnp.sum(squares, axis=1, keepdims=True) / (NT * features) + eps)
    for t in range(NT):
        normed[t] = (
            rows_all[t].astype(F32) * inverse * gain_ref[0:1, t * features:(t + 1) * features]
        ).astype(BF16)

    loads[3].wait()
    cosine, sine = angles[0], angles[1]
    depth = q_all.shape[3]

    def kv_part(yos, total):
        def add(xx, total):
            for yo in yos:
                row = lax.rem(y + yo + NY, NY)
                columns = pl.ds(pl.multiple_of(row * depth, depth), depth)
                total = total + jnp.dot(
                    normed[xx, :, columns], kv_all[0, xx, row], preferred_element_type=F32
                ) + jnp.dot(normed[NX + xx, :, columns], kv_all[1, xx, row], preferred_element_type=F32)
            return total

        return lax.fori_loop(0, NX, add, total)

    early[...] = kv_part((0, -1, 1, -2, 2, -3, 3), jnp.zeros((rows, kv_all.shape[-1]), F32))
    kv_hop(4)
    keyval = kv_part((-4,), early[...])
    span_kv[spot] = jnp.concatenate(
        [turned(keyval[:, :HD], cosine, sine), keyval[:, HD:]], axis=1
    ).astype(BF16)
    shared = [
        push(span_kv.at[spot], span_kv.at[spot], span_kv.at[place], (me - spot + place, tp))
        for place in line
    ]

    loads[1].wait()
    q_sum[...] = jnp.zeros_like(q_sum)

    def q_part(yo):
        low = 1 if yo < -3 else 0
        for other in (0, 1):
            off = 4 if low and other else yo
            for way, xo in ((X_RIGHT, -1), (X_LEFT, 1), (X_RIGHT if other == 0 else X_LEFT, -2 if other == 0 else 2)):
                key = (id(q_all), way, other, xo, off)
                if key in table:
                    arrived(q_all, way, other, xo, off)
        row = lax.rem(y + yo + NY, NY)
        columns = pl.ds(pl.multiple_of(row * depth, depth), depth)

        def add(xx, carry):
            q_sum[...] += jnp.dot(
                normed[xx, :, columns], q_all[0, xx, row], preferred_element_type=F32
            ) + jnp.dot(normed[NX + xx, :, columns], q_all[1, xx, row], preferred_element_type=F32)
            return carry

        lax.fori_loop(0, NX, add, 0)

    for yo in (0, -1, 1, -2, 2, -3, 3, -4):
        q_part(yo)

    for copy in shared:
        copy.wait_recv()
    span = LINE * rows
    keys = span_kv[:, :, :HD].reshape(span, HD)
    values = span_kv[:, :, HD:].reshape(span, HD)
    position = lax.broadcasted_iota(jnp.int32, (rows, span), 0) + spot * rows
    causal = position >= lax.broadcasted_iota(jnp.int32, (rows, span), 1)
    factor = math.log2(math.e) / math.sqrt(HD)
    for head in range(q_sum.shape[1] // HD):
        lanes = slice(head * HD, (head + 1) * HD)
        rot_query = turned(q_sum[:, lanes], cosine, sine).astype(BF16)
        scores = lax.dot_general(rot_query, keys, (((1,), (1,)), ((), ())), preferred_element_type=F32)
        scores = jnp.where(causal, scores, -jnp.inf)
        weights = jnp.exp2((scores - jnp.max(scores, axis=1, keepdims=True)) * factor)
        weights = (weights * (1.0 / jnp.sum(weights, axis=1, keepdims=True))).astype(BF16)
        out_ref[:, lanes] = jnp.dot(weights, values, preferred_element_type=F32).astype(BF16)

    assert not table
    for copy in copies:
        copy.wait_send()


def local(angles, hidden, keep_first, keep_second, norm_gain, w_query, w_keyval):
    rows = keep_second.shape[0]
    depth, q_cols = w_query.shape
    kv_cols = 2 * w_keyval.shape[2]
    span, features = hidden.shape
    choices = keep_first.shape[1]
    vmem = pl.BlockSpec(memory_space=pltpu.VMEM)
    away = pl.BlockSpec(memory_space=pl.ANY)
    return pl.pallas_call(
        kernel,
        out_shape=jax.ShapeDtypeStruct((rows, q_cols), BF16),
        in_specs=[away, vmem, vmem, vmem, away, vmem, away],
        out_specs=vmem,
        scratch_shapes=[
            pltpu.VMEM((depth, kv_cols), BF16),
            pltpu.VMEM((2, NX, NY, depth, q_cols), BF16),
            pltpu.VMEM((2, NX, NY, depth, kv_cols), BF16),
            pltpu.VMEM((span, features), BF16),
            pltpu.VMEM((choices, features), BF16),
            pltpu.VMEM((1, rows), jnp.int32),
            pltpu.VMEM((rows, features), BF16),
            pltpu.VMEM((rows, features), BF16),
            pltpu.VMEM((NT, rows, features), BF16),
            pltpu.VMEM((NT, rows, features), BF16),
            pltpu.VMEM((2, rows, HD), F32),
            pltpu.VMEM((rows, q_cols), F32),
            pltpu.VMEM((rows, kv_cols), F32),
            pltpu.VMEM((LINE, rows, kv_cols), BF16),
            pltpu.SemaphoreType.DMA((COPIES,)),
            pltpu.SemaphoreType.DMA((COPIES,)),
            pltpu.SemaphoreType.DMA((4,)),
        ],
        compiler_params=pltpu.CompilerParams(
            collective_id=0, has_side_effects=True, vmem_limit_bytes=56 * 1024 * 1024
        ),
        cost_estimate=pl.CostEstimate(flops=7_000_000_000, bytes_accessed=20_000_000, transcendentals=1_000_000),
    )(
        hidden, keep_first, keep_second.reshape(1, rows), norm_gain.reshape(1, -1), w_query,
        w_keyval, angles,
    )


def rotary_tables(length):
    spread = np.exp(np.arange(HD // 2, dtype=np.float32) * np.float32(-2.0 * math.log(10000.0) / HD))
    turn = np.arange(length, dtype=np.float32)[:, None] * spread.astype(np.float32)[None, :]
    cosine, sine = np.cos(turn.astype(np.float64)), np.sin(turn.astype(np.float64))
    return np.stack(
        [np.concatenate([cosine, cosine], axis=1), np.concatenate([-sine, sine], axis=1)]
    ).astype(np.float32)


def solution(mesh):
    placed = (P("seq", "tp"), P("seq", None), P("seq"), P(), P("seq", "tp"), P("seq", None, "tp"))
    tables = rotary_tables(1024)

    def run(*args):
        return jax.shard_map(
            local, mesh=mesh, in_specs=(P(),) + placed, out_specs=P("seq", "tp"), check_vma=False
        )(jnp.asarray(tables), *args)

    return run
```

```python
import functools
import math

import jax
import jax.numpy as jnp
import numpy as np
from jax import lax
from jax.experimental import pallas as pl
from jax.experimental.pallas import tpu as pltpu
from jax.sharding import PartitionSpec as P

HD = 128
NX, NY, NZ = 4, 8, 4
LINE = 4
NT = 2 * NZ
MESH = pl.DeviceIdType.MESH
X_RIGHT, X_LEFT, Y_RIGHT, Y_LEFT, Z_OTHER = (1, 0, 0), (-1, 0, 0), (0, 1, 0), (0, -1, 0), (0, 0, 1)
COPIES = 97
BF16, F32 = jnp.bfloat16, jnp.float32

eps = 1e-05


def one_hot(picks, first, count):
    n = picks.shape[1]
    down = jnp.transpose(jnp.broadcast_to(picks, (128, n))) - first
    lane = lax.broadcasted_iota(jnp.int32, (n, 128), 1)
    return jnp.concatenate(
        [jnp.where(down == lane + start, 1.0, 0.0).astype(BF16) for start in range(0, count, 128)], axis=1
    )


def turned(values, cosine, sine):
    return values * cosine + pltpu.roll(values, HD // 2, 1) * sine


def kernel(
    hidden_ref, keep_ref, picks_ref, gain_ref, wq_ref, wkv_in, angles_ref, out_ref,
    wkv_ref, q_all, kv_all, hidden, kept, others, outgoing, incoming, rows_all, normed, angles, q_sum, early, span_kv,
    send_sems, recv_sems, local_sems,
):
    me = lax.axis_index("seq")
    tp = lax.axis_index("tp")
    zl, x, y = me // (NX * NY), me // NY % NX, me % NY
    zh, core = tp // 2, tp % 2
    odd = me % 2
    spot = me % LINE
    rows = picks_ref.shape[1]
    half = rows // 2
    features = hidden_ref.shape[1]
    choices = keep_ref.shape[1]

    def device(way):
        dx, dy, dz = way
        nx, ny, nz = lax.rem(x + dx + NX, NX), lax.rem(y + dy + NY, NY), lax.rem(zl + dz, 2)
        return (nz * (NX * NY) + nx * NY + ny, tp)

    def slot(dz, other):
        return lax.rem(zh + dz + NZ, NZ) * 2 + (1 - core if other else core)

    mate = (me + 1 - 2 * odd, tp)
    sibling = (me, tp + 1 - 2 * core)
    above, below = (me, slot(1, False)), (me, slot(-1, False))
    line = [
        lax.rem(spot // 2 * 2 + 1 - spot % 2, LINE),
        lax.rem(spot + 2, LINE),
        LINE - 1 - spot,
    ]

    def at(ref, other, xo, yo):
        plane = lax.rem(zl + other, 2)
        row = lax.rem(y + yo + 2 * NY, NY)
        if xo is None:
            return ref.at[plane, :, row]
        return ref.at[plane, lax.rem(x + xo + 2 * NX, NX), row]

    wkv_ref[...] = jnp.concatenate([wkv_in[:, 0, :], wkv_in[:, 1, :]], axis=1)
    loads = [
        pltpu.make_async_copy(hidden_ref, hidden, local_sems.at[0]),
        pltpu.make_async_copy(wq_ref, at(q_all, 0, 0, 0), local_sems.at[1]),
        pltpu.make_async_copy(wkv_ref, at(kv_all, 0, 0, 0), local_sems.at[2]),
        pltpu.make_async_copy(angles_ref.at[:, pl.ds(pl.multiple_of(spot * rows, rows), rows)], angles, local_sems.at[3]),
    ]
    for load in loads:
        load.start()

    barrier = pltpu.get_barrier_semaphore()
    partners = [device(way) for way in (X_RIGHT, X_LEFT, Y_RIGHT, Y_LEFT, Z_OTHER)]
    partners += [sibling, above, below] + [(me - spot + line[1], tp), (me - spot + line[2], tp)]
    for partner in partners:
        pl.semaphore_signal(barrier, inc=1, device_id=partner, device_id_type=MESH)
    pl.semaphore_wait(barrier, len(partners))

    copies = []
    table = {}

    def push(src, dst, landing, where):
        number = len(copies)
        copy = pltpu.make_async_remote_copy(
            src_ref=src, dst_ref=dst, send_sem=send_sems.at[number], recv_sem=recv_sems.at[number],
            device_id=where, device_id_type=MESH,
        )
        copy.start()
        copies.append(copy)
        return pltpu.make_async_remote_copy(
            src_ref=landing, dst_ref=landing, send_sem=send_sems.at[number], recv_sem=recv_sems.at[number],
            device_id=where, device_id_type=MESH,
        )

    def send(ref, way, other, xo, yo, src=None):
        dst = at(ref, other, xo, yo)
        dx, dy, dz = way
        there = (other + dz) % 2, None if xo is None else xo - dx, yo - dy
        table[(id(ref), way) + there] = push(dst if src is None else src, dst, at(ref, *there), device(way))

    def arrived(ref, way, other, xo, yo):
        table.pop((id(ref), way, other, xo, yo)).wait_recv()

    picks_in = push(picks_ref, others, others, mate)
    send(kv_all, Z_OTHER, 0, 0, 0, wkv_ref)
    send(q_all, Z_OTHER, 0, 0, 0, wq_ref)
    for way in (X_RIGHT, X_LEFT):
        send(kv_all, way, 0, 0, 0, wkv_ref)
    for way in (Y_RIGHT, Y_LEFT):
        send(q_all, way, 0, 0, 0, wq_ref)
    for way in (X_RIGHT, X_LEFT):
        send(q_all, way, 0, 0, 0, wq_ref)

    first_hot = one_hot(keep_ref[...], 0, hidden.shape[0])
    loads[0].wait()
    kept[...] = jnp.dot(first_hot, hidden[...], preferred_element_type=F32).astype(BF16)
    picks_in.wait_recv()
    outgoing[...] = jnp.dot(
        one_hot(others[...], odd * choices, choices), kept[...], preferred_element_type=F32
    ).astype(BF16)
    rows_in = push(outgoing, incoming, incoming, mate)

    arrived(kv_all, Z_OTHER, 1, 0, 0)
    for way in (X_RIGHT, X_LEFT):
        send(kv_all, way, 1, 0, 0)
    arrived(q_all, Z_OTHER, 1, 0, 0)
    for way in (Y_RIGHT, Y_LEFT):
        send(q_all, way, 1, 0, 0)
    for way in (X_RIGHT, X_LEFT):
        send(q_all, way, 1, 0, 0)
    own_rows = jnp.dot(
        one_hot(picks_ref[...], odd * choices, choices), kept[...], preferred_element_type=F32
    ).astype(BF16)
    rows_all[tp] = own_rows
    arrived(kv_all, X_RIGHT, 0, -1, 0)
    send(kv_all, X_RIGHT, 0, -1, 0)
    arrived(kv_all, X_LEFT, 1, 1, 0)
    send(kv_all, X_LEFT, 1, 1, 0)
    arrived(kv_all, X_LEFT, 0, 1, 0)
    arrived(kv_all, X_RIGHT, 1, -1, 0)
    loads[2].wait()

    def second_hop(yo):
        arrived(q_all, X_RIGHT, 0, -1, yo)
        send(q_all, X_RIGHT, 0, -1, yo)
        arrived(q_all, X_LEFT, 1, 1, yo)
        send(q_all, X_LEFT, 1, 1, yo)

    def kv_hop(step):
        if step == 0:
            arrived(kv_all, X_RIGHT, 0, -2, 0)
            arrived(kv_all, X_LEFT, 1, 2, 0)
            for way in (Y_RIGHT, Y_LEFT):
                for other in (0, 1):
                    send(kv_all, way, other, None, 0)
            return
        for other in (0, 1):
            for way, sign, far in ((Y_RIGHT, -1, 4 - other), (Y_LEFT, 1, 3 + other)):
                if step <= far:
                    arrived(kv_all, way, other, None, sign * step)
                    if step < far:
                        send(kv_all, way, other, None, sign * step)

    def q_hop(step):
        for other in (0, 1):
            for way, sign, far in ((Y_RIGHT, -1, 4 - other), (Y_LEFT, 1, 3 + other)):
                if step <= far:
                    arrived(q_all, way, other, 0, sign * step)
                    if step < far:
                        send(q_all, way, other, 0, sign * step)
                    for side in (X_RIGHT, X_LEFT):
                        send(q_all, side, other, 0, sign * step)

    def block(dz, other, part=None):
        ref = rows_all.at[slot(dz, other)]
        if part is None:
            return ref
        return ref.at[pl.ds(part * half, half)]

    q_hop(1)
    kv_hop(0)
    rows_in.wait_recv()
    rows_all[tp] = rows_all[tp] + incoming[...]
    mine = block(0, False)
    to_above = push(mine, mine, block(-1, False), above)
    to_below = push(mine, mine, block(1, False), below)
    crossed = [push(mine, mine, block(0, True), sibling)]
    second_hop(0)
    q_hop(2)
    second_hop(-1)
    second_hop(1)
    kv_hop(1)
    q_hop(3)
    second_hop(-2)
    to_above.wait_recv()
    far_above = push(block(-1, False, 0), block(-1, False, 0), block(2, False, 0), above)
    to_below.wait_recv()
    far_below = push(block(1, False, 1), block(1, False, 1), block(2, False, 1), below)
    crossed.append(push(block(-1, False), block(-1, False), block(-1, True), sibling))
    crossed.append(push(block(1, False), block(1, False), block(1, True), sibling))
    kv_hop(2)
    second_hop(2)
    for other, way, sign in ((0, Y_RIGHT, -1), (1, Y_LEFT, 1)):
        arrived(q_all, way, other, 0, sign * 4)
        for side in (X_RIGHT, X_LEFT):
            send(q_all, side, other, 0, sign * 4)
    second_hop(-3)
    far_above.wait_recv()
    far_below.wait_recv()
    crossed.append(push(block(2, False), block(2, False), block(2, True), sibling))
    kv_hop(3)
    second_hop(3)
    arrived(q_all, X_RIGHT, 0, -1, -4)
    send(q_all, X_RIGHT, 0, -1, -4)
    arrived(q_all, X_LEFT, 1, 1, 4)
    send(q_all, X_LEFT, 1, 1, 4)

    for copy in crossed:
        copy.wait_recv()
    squares = jnp.zeros((rows, 128), F32)
    for t in range(NT):
        wide = rows_all[t].astype(F32)
        wide = wide * wide
        for start in range(0, features, 128):
            squares = squares + wide[:, start:start + 128]
    inverse = lax.rsqrt(jnp.sum(squares, axis=1, keepdims=True) / (NT * features) + eps)
    for t in range(NT):
        normed[t] = (
            rows_all[t].astype(F32) * inverse * gain_ref[0:1, t * features:(t + 1) * features]
        ).astype(BF16)

    loads[3].wait()
    cosine, sine = angles[0], angles[1]
    depth = q_all.shape[3]

    def kv_part(yos, total):
        def add(xx, total):
            for yo in yos:
                row = lax.rem(y + yo + NY, NY)
                columns = pl.ds(pl.multiple_of(row * depth, depth), depth)
                total = total + jnp.dot(
                    normed[xx, :, columns], kv_all[0, xx, row], preferred_element_type=F32
                ) + jnp.dot(normed[NX + xx, :, columns], kv_all[1, xx, row], preferred_element_type=F32)
            return total

        return lax.fori_loop(0, NX, add, total)

    early[...] = kv_part((0, -1, 1, -2, 2, -3, 3), jnp.zeros((rows, kv_all.shape[-1]), F32))
    kv_hop(4)
    keyval = kv_part((-4,), early[...])
    span_kv[spot] = jnp.concatenate(
        [turned(keyval[:, :HD], cosine, sine), keyval[:, HD:]], axis=1
    ).astype(BF16)
    shared = [
        push(span_kv.at[spot], span_kv.at[spot], span_kv.at[place], (me - spot + place, tp))
        for place in line
    ]

    loads[1].wait()
    q_sum[...] = jnp.zeros_like(q_sum)

    def q_part(yo):
        low = 1 if yo < -3 else 0
        for other in (0, 1):
            off = 4 if low and other else yo
            for way, xo in ((X_RIGHT, -1), (X_LEFT, 1), (X_RIGHT if other == 0 else X_LEFT, -2 if other == 0 else 2)):
                key = (id(q_all), way, other, xo, off)
                if key in table:
                    arrived(q_all, way, other, xo, off)

    def q_rows(yos):
        for yo in yos:
            q_part(yo)

        def add(xx, total):
            for yo in yos:
                row = lax.rem(y + yo + NY, NY)
                columns = pl.ds(pl.multiple_of(row * depth, depth), depth)
                total = total + jnp.dot(
                    normed[xx, :, columns], q_all[0, xx, row], preferred_element_type=F32
                ) + jnp.dot(normed[NX + xx, :, columns], q_all[1, xx, row], preferred_element_type=F32)
            return total

        q_sum[...] = lax.fori_loop(0, NX, add, q_sum[...])

    q_rows((0, -1, 1, -2, 2, -3))
    q_rows((3, -4))

    for copy in shared:
        copy.wait_recv()
    span = LINE * rows
    keys = span_kv[:, :, :HD].reshape(span, HD)
    values = span_kv[:, :, HD:].reshape(span, HD)
    position = lax.broadcasted_iota(jnp.int32, (rows, span), 0) + spot * rows
    causal = position >= lax.broadcasted_iota(jnp.int32, (rows, span), 1)
    factor = math.log2(math.e) / math.sqrt(HD)
    for head in range(q_sum.shape[1] // HD):
        lanes = slice(head * HD, (head + 1) * HD)
        rot_query = turned(q_sum[:, lanes], cosine, sine).astype(BF16)
        scores = lax.dot_general(rot_query, keys, (((1,), (1,)), ((), ())), preferred_element_type=F32)
        scores = jnp.where(causal, scores, -jnp.inf)
        weights = jnp.exp2((scores - jnp.max(scores, axis=1, keepdims=True)) * factor)
        weights = (weights * (1.0 / jnp.sum(weights, axis=1, keepdims=True))).astype(BF16)
        out_ref[:, lanes] = jnp.dot(weights, values, preferred_element_type=F32).astype(BF16)

    assert not table
    for copy in copies:
        copy.wait_send()


def local(angles, hidden, keep_first, keep_second, norm_gain, w_query, w_keyval):
    rows = keep_second.shape[0]
    depth, q_cols = w_query.shape
    kv_cols = 2 * w_keyval.shape[2]
    span, features = hidden.shape
    choices = keep_first.shape[1]
    vmem = pl.BlockSpec(memory_space=pltpu.VMEM)
    away = pl.BlockSpec(memory_space=pl.ANY)
    return pl.pallas_call(
        kernel,
        out_shape=jax.ShapeDtypeStruct((rows, q_cols), BF16),
        in_specs=[away, vmem, vmem, vmem, away, vmem, away],
        out_specs=vmem,
        scratch_shapes=[
            pltpu.VMEM((depth, kv_cols), BF16),
            pltpu.VMEM((2, NX, NY, depth, q_cols), BF16),
            pltpu.VMEM((2, NX, NY, depth, kv_cols), BF16),
            pltpu.VMEM((span, features), BF16),
            pltpu.VMEM((choices, features), BF16),
            pltpu.VMEM((1, rows), jnp.int32),
            pltpu.VMEM((rows, features), BF16),
            pltpu.VMEM((rows, features), BF16),
            pltpu.VMEM((NT, rows, features), BF16),
            pltpu.VMEM((NT, rows, features), BF16),
            pltpu.VMEM((2, rows, HD), F32),
            pltpu.VMEM((rows, q_cols), F32),
            pltpu.VMEM((rows, kv_cols), F32),
            pltpu.VMEM((LINE, rows, kv_cols), BF16),
            pltpu.SemaphoreType.DMA((COPIES,)),
            pltpu.SemaphoreType.DMA((COPIES,)),
            pltpu.SemaphoreType.DMA((4,)),
        ],
        compiler_params=pltpu.CompilerParams(
            collective_id=0, has_side_effects=True, vmem_limit_bytes=56 * 1024 * 1024
        ),
        cost_estimate=pl.CostEstimate(flops=7_000_000_000, bytes_accessed=20_000_000, transcendentals=1_000_000),
    )(
        hidden, keep_first, keep_second.reshape(1, rows), norm_gain.reshape(1, -1), w_query,
        w_keyval, angles,
    )


def rotary_tables(length):
    spread = np.exp(np.arange(HD // 2, dtype=np.float32) * np.float32(-2.0 * math.log(10000.0) / HD))
    turn = np.arange(length, dtype=np.float32)[:, None] * spread.astype(np.float32)[None, :]
    cosine, sine = np.cos(turn.astype(np.float64)), np.sin(turn.astype(np.float64))
    return np.stack(
        [np.concatenate([cosine, cosine], axis=1), np.concatenate([-sine, sine], axis=1)]
    ).astype(np.float32)


def solution(mesh):
    placed = (P("seq", "tp"), P("seq", None), P("seq"), P(), P("seq", "tp"), P("seq", None, "tp"))
    tables = rotary_tables(1024)

    def run(*args):
        return jax.shard_map(
            local, mesh=mesh, in_specs=(P(),) + placed, out_specs=P("seq", "tp"), check_vma=False
        )(jnp.asarray(tables), *args)

    return run
```
